32 devices in a mesh: tm: 4 (over y, x), slab: 8 (over z, core).
Axes of the slice: x: 2, y: 2, z: 4, core: 2. Of those that a mesh axis runs over, the one named last changes fastest.
Arguments:
- u_states: bfloat16 [4, 64, 32, 8, 256], P('tm', None, 'slab'), may hold values from -6 to 6
- lam_points: float32 [4, 64, 32, 8, 256], P('tm', None, 'slab'), may hold values from -6 to 6
- weight: bfloat16 [27, 64, 64], replicated, may hold values from -0.15625 to 0.15625
- bias: float32 [64], replicated, may hold values from -3 to 3
Outputs:
- lam_new: float32 [4, 64, 32, 8, 256], P('tm', None, 'slab')
- grad_w: float32 [27, 64, 64], replicated
- grad_b: float32 [64], replicated
The draws below stay inside these ranges and needn't reach their ends.
All inputs are finite; a program needn't handle non-finite values.
Results may differ from the reference program's by a relative error of at most 0.0065.
Values may be sent and summed in bfloat16 or wider, within the bound.
A program may use at most 256 MiB of HBM per device.

```python
import math
from functools import partial
import jax
import jax.numpy as jnp
from jax import lax

C = 64
CX = 8
CY = 256
GROUPS = 4
NZ = 32
N_TM = 4


def shard_levels(stream_key, shape, shards, low, high):
    loudness = 1.0
    for dim, parts in shards:
        steps = jax.random.uniform(jax.random.fold_in(jax.random.fold_in(stream_key, 6), dim), (parts,), jnp.float32, low / len(shards), high / len(shards))
        loudness = loudness * jnp.repeat(jnp.exp(steps), shape[dim] // parts).reshape((-1,) + (1,) * (len(shape) - 1 - dim))
    return loudness


def noise(rng, dims, spread, limit, cuts=(), kind=jnp.bfloat16):
    entries = spread * jax.random.normal(rng, dims, jnp.float32)
    if cuts:
        entries = entries * shard_levels(rng, dims, cuts, -0.22, 0.18)
    return jnp.clip(entries, -limit, limit).astype(kind)


def setup_inputs(seed: int = 0) -> dict:
    arg_keys = jax.random.split(jax.random.key(seed), 5)
    return {
        "u_states": noise(arg_keys[0], (GROUPS, C, NZ, CX, CY), 1.0, 6.0, ((0, 4), (2, 8))),
        "lam_points": noise(arg_keys[1], (GROUPS, C, NZ, CX, CY), 1.0, 6.0, ((0, 4), (2, 8)), jnp.float32),
        "weight": noise(arg_keys[2], (27, C, C), (27 * C) ** -0.5, 0.15625),
        "bias": noise(arg_keys[3], (C,), 0.5, 3.0, (), jnp.float32),
    }


step_size = 0.25

def correlate(field, kernel):
    return lax.conv_general_dilated(field[None], kernel, (1, 1, 1), ((1, 1), (1, 1), (1, 1)), dimension_numbers=('NCDHW', 'OIDHW', 'NCDHW'), precision=lax.Precision.HIGHEST)[0]

def restrict(field):
    shaped = field.reshape(field.shape[0], field.shape[1], field.shape[2] // 2, 2, field.shape[3] // 2, 2)
    return lax.optimization_barrier(jnp.mean(shaped, axis=(3, 5)))

def prolong(field):
    return jnp.repeat(jnp.repeat(field, 2, axis=2), 2, axis=3)

def rounded(value):
    return lax.optimization_barrier(value.astype(jnp.bfloat16)).astype(jnp.float32)

def group_pass(kernel, bias, diagonal, inputs):
    state_zero, adjoint = inputs
    offset = bias[:, None, None, None]
    start = state_zero.astype(jnp.float32)
    tanh_zero = jnp.tanh(correlate(start, kernel) + offset)
    sens_zero = 1.0 - tanh_zero * tanh_zero
    state_one = rounded(start + step_size * tanh_zero)
    tanh_one = jnp.tanh(correlate(state_one, kernel) + offset)
    sens_one = 1.0 - tanh_one * tanh_one
    cot_one = rounded(sens_one * adjoint)
    _, pull_one = jax.vjp(correlate, state_one, kernel)
    back_one, kgrad_one = pull_one(cot_one)
    middle = adjoint + step_size * back_one
    cot_zero = rounded(sens_zero * middle)
    _, pull_zero = jax.vjp(correlate, start, kernel)
    back_zero, kgrad_zero = pull_zero(cot_zero)
    fine_back = middle + step_size * back_zero
    factor = 1.0 + 2.0 * step_size * diagonal[:, None, None, None] * restrict(sens_zero)
    bias_grad = lax.optimization_barrier(jnp.sum(cot_zero + cot_one, axis=(1, 2, 3)))
    return (restrict(fine_back), factor, kgrad_zero + kgrad_one, bias_grad)

def descend(earlier, inputs):
    value = inputs[0] * earlier + inputs[1]
    return (value, value)

def reference(u_states, lam_points, weight, bias):
    kernel = weight.astype(jnp.float32).reshape(3, 3, 3, C, C).transpose(3, 4, 0, 1, 2)
    diagonal = jnp.diagonal(weight[13]).astype(jnp.float32)
    coarse_back, factor, kgrad, bias_grad = lax.map(partial(group_pass, kernel, bias, diagonal), (u_states, lam_points))
    zero_block = jnp.zeros_like(coarse_back[:1])
    rest = jnp.concatenate([zero_block, coarse_back[:-1]], 0) - jax.vmap(restrict)(lam_points)
    factor_prev = jnp.concatenate([zero_block, factor[:-1]], 0)
    _, correction = lax.scan(descend, jnp.zeros_like(rest[0]), (factor_prev, rest))
    lam_new = lam_points + jax.vmap(prolong)(correction)
    grad_scale = step_size / math.sqrt(2 * N_TM * NZ * CX * CY)
    grad_w = grad_scale * lax.optimization_barrier(jnp.sum(kgrad, 0)).transpose(2, 3, 4, 0, 1).reshape(27, C, C)
    grad_b = grad_scale * lax.optimization_barrier(jnp.sum(bias_grad, 0))
    return (lam_new, grad_w, grad_b)
```

```python
import functools
import math

import jax
import jax.numpy as jnp
from jax import lax
from jax.experimental import pallas as pl
from jax.experimental.pallas import tpu as pltpu
from jax.sharding import PartitionSpec as P

step_size = 0.25
MESH = pl.DeviceIdType.MESH
f32 = jnp.float32
bf16 = jnp.bfloat16


def banded(taps):
    channels = taps.shape[1]
    ordered = taps.reshape(3, 3, 3, channels, channels).transpose(0, 2, 3, 1, 4)
    rows = ordered.reshape(3, 3, channels, 3 * channels)
    upper = jnp.pad(rows, ((0, 0), (0, 0), (0, 0), (0, channels)))
    lower = jnp.pad(rows, ((0, 0), (0, 0), (0, 0), (channels, 0)))
    return jnp.concatenate([upper, lower], 2).reshape(9, 2 * channels, 4 * channels)


def kernel(
    n_tm, n_slab, chunk,
    u_ref, lam_ref, wf_ref, wb_ref, bias_ref, diag_ref, down_ref, up_ref,
    new_ref, grad_ref,
    v0, v1, g1, g0, halo, sens0, mid, gacc, bacc,
    early, late, early_in, late_in, gsend, rs_in, tm_all, total,
    halo_send, halo_recv, early_send, early_recv, late_send, late_recv,
    rs_send, rs_recv, tm_send, tm_recv, ag_send, ag_recv,
):
    planes, rows, cells = u_ref.shape
    channels = rows // 8
    pair = 2 * channels
    pairs = rows // pair
    me_tm = lax.axis_index("tm")
    me = lax.axis_index("slab")

    def slab_peer(d):
        return lax.rem(me + d, n_slab)

    def tm_peer(d):
        return lax.rem(me_tm + d, n_tm)

    barrier = pltpu.get_barrier_semaphore()
    for d in range(1, n_slab):
        pl.semaphore_signal(barrier, inc=1, device_id={"slab": slab_peer(d)}, device_id_type=MESH)
    for d in range(1, n_tm):
        pl.semaphore_signal(barrier, inc=1, device_id={"tm": tm_peer(d)}, device_id_type=MESH)

    lane = lax.broadcasted_iota(jnp.int32, (pair, cells), 1)

    def put(buf, z, j, value):
        at = pl.ds(pl.multiple_of(channels + j * pair, channels), pair)
        wide = value.astype(f32)
        buf[1, z, at, :] = value
        buf[0, z, at, :] = jnp.where(lane == 0, 0.0, pltpu.roll(wide, 1, 1)).astype(bf16)
        buf[2, z, at, :] = jnp.where(lane == cells - 1, 0.0, pltpu.roll(wide, cells - 1, 1)).astype(bf16)

    def group(j):
        return pl.ds(pl.multiple_of(j * pair, pair), pair)

    def exchange(e, buf, start):
        own = pl.ds(channels, rows)

        def up():
            return pltpu.make_async_remote_copy(
                src_ref=buf.at[1, planes, own], dst_ref=halo.at[e, 0],
                send_sem=halo_send.at[e, 0], recv_sem=halo_recv.at[e, 0],
                device_id={"slab": jnp.minimum(me + 1, n_slab - 1)}, device_id_type=MESH)

        def down():
            return pltpu.make_async_remote_copy(
                src_ref=buf.at[1, 1, own], dst_ref=halo.at[e, 1],
                send_sem=halo_send.at[e, 1], recv_sem=halo_recv.at[e, 1],
                device_id={"slab": jnp.maximum(me - 1, 0)}, device_id_type=MESH)

        if start:
            @pl.when(me < n_slab - 1)
            def _():
                up().start()

            @pl.when(me > 0)
            def _():
                down().start()
        else:
            @pl.when(me > 0)
            def _():
                up().wait_recv()

                def move(j, carry):
                    put(buf, 0, j, halo[e, 0, group(j), :])
                    return carry
                lax.fori_loop(0, pairs, move, 0)

            @pl.when(me == 0)
            def _():
                buf[:, 0, :, :] = jnp.zeros_like(buf[:, 0, :, :])

            @pl.when(me < n_slab - 1)
            def _():
                down().wait_recv()

                def move(j, carry):
                    put(buf, planes + 1, j, halo[e, 1, group(j), :])
                    return carry
                lax.fori_loop(0, pairs, move, 0)

            @pl.when(me == n_slab - 1)
            def _():
                buf[:, planes + 1, :, :] = jnp.zeros_like(buf[:, planes + 1, :, :])

            @pl.when(me < n_slab - 1)
            def _():
                up().wait_send()

            @pl.when(me > 0)
            def _():
                down().wait_send()

    def conv(buf, taps, first, stride, count, finish):
        def body(k, carry):
            z = first + (k // pairs) * stride
            j = lax.rem(k, pairs)
            window = pl.ds(pl.multiple_of(j * pair, pair), 2 * pair)
            acc = jnp.zeros((pair, cells), f32)
            for a in range(3):
                for c in range(3):
                    acc = acc + jnp.dot(taps[3 * a + c], buf[c, z + a, window, :],
                                        preferred_element_type=f32)
            finish(z, j, acc)
            return carry
        lax.fori_loop(0, count * pairs, body, 0)

    def inner(buf, taps, finish):
        if planes > 2:
            conv(buf, taps, 1, 1, planes - 2, finish)

    def outer(buf, taps, finish):
        conv(buf, taps, 0, planes - 1, 2, finish)

    def taps_grad(cot, buf):
        for a in range(3):
            for c in range(3):
                def body(k, carry, a=a, c=c):
                    j = k
                    window = pl.ds(pl.multiple_of(j * pair, pair), 2 * pair)
                    at = pl.ds(pl.multiple_of(channels + j * pair, channels), pair)
                    acc = gacc[3 * a + c]
                    for z in range(planes):
                        acc = acc + lax.dot_general(
                            cot[1, z + 1, at, :], buf[c, z + a, window, :],
                            (((1,), (1,)), ((), ())), preferred_element_type=f32)
                    gacc[3 * a + c] = acc
                    return carry
                lax.fori_loop(0, pairs, body, 0)

    def restricted(value):
        summed = (value[:channels] + value[channels:]).astype(bf16)
        return jnp.dot(summed, down_ref[...], preferred_element_type=f32)

    def half(j):
        return pl.ds(pl.multiple_of(j * channels, channels), channels)

    def load_u(k, carry):
        j = lax.rem(k, pairs)
        z = k // pairs
        put(v0, z + 1, j, u_ref[z, group(j), :])
        return carry
    lax.fori_loop(0, planes * pairs, load_u, 0)

    pl.semaphore_wait(barrier, n_slab - 1 + n_tm - 1)
    exchange(0, v0, True)

    for buf in (v0, v1, g1, g0):
        for c in range(3):
            for z in range(planes + 2):
                buf[c, z, :channels, :] = jnp.zeros((channels, cells), bf16)
                buf[c, z, channels + rows:, :] = jnp.zeros((channels, cells), bf16)
    gacc[...] = jnp.zeros_like(gacc)
    bacc[...] = jnp.zeros_like(bacc)

    def after_first(z, j, acc):
        th = jnp.tanh(acc + bias_ref[...])
        sens = 1.0 - th * th
        sens0[z, group(j), :] = sens
        state = (u_ref[z, group(j), :].astype(f32) + step_size * th).astype(bf16)
        put(v1, z + 1, j, state)
        early[0, z, half(j), :] = (1.0 + 2.0 * step_size * diag_ref[...] * restricted(sens)).astype(bf16)
        early[1, z, half(j), :] = restricted(lam_ref[z, group(j), :]).astype(bf16)

    inner(v0, wf_ref, after_first)
    exchange(0, v0, False)
    outer(v0, wf_ref, after_first)
    exchange(1, v1, True)

    def to_later(src, dst, send, recv, d):
        return pltpu.make_async_remote_copy(
            src_ref=src, dst_ref=dst.at[d - 1], send_sem=send.at[d - 1], recv_sem=recv.at[d - 1],
            device_id={"tm": jnp.minimum(me_tm + d, n_tm - 1)}, device_id_type=MESH)

    for d in range(1, n_tm):
        @pl.when(me_tm + d < n_tm)
        def _(d=d):
            to_later(early, early_in, early_send, early_recv, d).start()

    def after_second(z, j, acc):
        th = jnp.tanh(acc + bias_ref[...])
        cot = ((1.0 - th * th) * lam_ref[z, group(j), :]).astype(bf16)
        bacc[...] += cot.astype(f32)
        put(g1, z + 1, j, cot)

    inner(v1, wf_ref, after_second)
    exchange(1, v1, False)
    outer(v1, wf_ref, after_second)
    exchange(2, g1, True)
    taps_grad(g1, v1)

    def after_third(z, j, acc):
        middle = lam_ref[z, group(j), :] + step_size * acc
        mid[z, group(j), :] = middle
        cot = (sens0[z, group(j), :] * middle).astype(bf16)
        bacc[...] += cot.astype(f32)
        put(g0, z + 1, j, cot)

    inner(g1, wb_ref, after_third)
    exchange(2, g1, False)
    outer(g1, wb_ref, after_third)
    exchange(3, g0, True)
    taps_grad(g0, v0)

    three = 3 * channels
    for t in range(9):
        block = gacc[t, :channels, :three] + gacc[t, channels:, channels:]
        gsend[t * channels:(t + 1) * channels, :three] = block.astype(bf16)
        side = jnp.zeros((channels, channels), f32)
        if t == 0:
            column = jnp.sum(bacc[:channels] + bacc[channels:], axis=1, keepdims=True)
            side = side + column
        gsend[t * channels:(t + 1) * channels, three:] = side.astype(bf16)
    padding = n_slab * chunk - 9 * channels
    if padding:
        gsend[9 * channels:, :] = jnp.zeros((padding, 4 * channels), bf16)

    def part(index):
        return pl.ds(pl.multiple_of(index * chunk, 16), chunk)

    def scatter(d):
        return pltpu.make_async_remote_copy(
            src_ref=gsend.at[part(slab_peer(d))], dst_ref=rs_in.at[d - 1],
            send_sem=rs_send.at[d - 1], recv_sem=rs_recv.at[d - 1],
            device_id={"slab": slab_peer(d)}, device_id_type=MESH)

    for d in range(1, n_slab):
        scatter(d).start()

    def after_fourth(z, j, acc):
        back = mid[z, group(j), :] + step_size * acc
        late[z, half(j), :] = restricted(back).astype(bf16)

    inner(g0, wb_ref, after_fourth)
    exchange(3, g0, False)
    outer(g0, wb_ref, after_fourth)

    for d in range(1, n_tm):
        @pl.when(me_tm + d < n_tm)
        def _(d=d):
            to_later(late, late_in, late_send, late_recv, d).start()

    mine = gsend[part(me), :].astype(f32)
    for d in range(1, n_slab):
        scatter(d).wait_recv()
        mine = mine + rs_in[d - 1].astype(f32)
    tm_all[me_tm] = mine.astype(bf16)

    def across(d):
        return pltpu.make_async_remote_copy(
            src_ref=tm_all.at[me_tm], dst_ref=tm_all.at[me_tm],
            send_sem=tm_send.at[d - 1], recv_sem=tm_recv.at[d - 1],
            device_id={"tm": tm_peer(d)}, device_id_type=MESH)

    for d in range(1, n_tm):
        across(d).start()
    for d in range(1, n_tm):
        across(d).wait_recv()
    whole = tm_all[0].astype(f32)
    for k in range(1, n_tm):
        whole = whole + tm_all[k].astype(f32)
    total[me] = whole.astype(bf16)

    def spread(d):
        return pltpu.make_async_remote_copy(
            src_ref=total.at[me], dst_ref=total.at[me],
            send_sem=ag_send.at[d - 1], recv_sem=ag_recv.at[d - 1],
            device_id={"slab": slab_peer(d)}, device_id_type=MESH)

    for d in range(1, n_slab):
        spread(d).start()

    for d in range(1, n_tm):
        @pl.when(me_tm >= d)
        def _(d=d):
            to_later(early, early_in, early_send, early_recv, d).wait_recv()
            to_later(late, late_in, late_send, late_recv, d).wait_recv()

    for d in range(n_tm):
        @pl.when(me_tm == d)
        def _(d=d):
            def body(k, carry):
                z = k // pairs
                j = lax.rem(k, pairs)
                at = half(j)
                first = early if d == 0 else early_in.at[d - 1]
                value = -first[1, z, at, :].astype(f32)
                for s in range(d, 0, -1):
                    lam_next = (early if s == 1 else early_in.at[s - 2])[1, z, at, :]
                    value = (early_in[s - 1, 0, z, at, :].astype(f32) * value
                             + late_in[s - 1, z, at, :].astype(f32) - lam_next.astype(f32))
                high = value.astype(bf16)
                low = (value - high.astype(f32)).astype(bf16)
                fine = (jnp.dot(high, up_ref[...], preferred_element_type=f32)
                        + jnp.dot(low, up_ref[...], preferred_element_type=f32))
                new_ref[z, group(j), :] = lam_ref[z, group(j), :] + jnp.concatenate([fine, fine], 0)
                return carry
            lax.fori_loop(0, planes * pairs, body, 0)

    for d in range(1, n_slab):
        spread(d).wait_recv()
    for s in range(n_slab):
        grad_ref[s] = total[s].astype(f32)

    for d in range(1, n_slab):
        scatter(d).wait_send()
        spread(d).wait_send()
    for d in range(1, n_tm):
        across(d).wait_send()

        @pl.when(me_tm + d < n_tm)
        def _(d=d):
            to_later(early, early_in, early_send, early_recv, d).wait_send()
            to_later(late, late_in, late_send, late_recv, d).wait_send()


def on_device(u_states, lam_points, weight, bias):
    n_tm, n_slab = lax.axis_size("tm"), lax.axis_size("slab")
    _, channels, planes, extent_x, cells = u_states.shape
    rows = channels * extent_x
    chunk = 16 * -(-9 * channels // (16 * n_slab))
    state = u_states[0].transpose(1, 2, 0, 3).reshape(planes, rows, cells)
    adjoint = lam_points[0].transpose(1, 2, 0, 3).reshape(planes, rows, cells)
    forward = banded(weight)
    backward = banded(weight[::-1].transpose(0, 2, 1))
    offset = jnp.tile(bias, 2)[:, None]
    diagonal = jnp.diagonal(weight[13]).astype(f32)[:, None]
    fine = lax.broadcasted_iota(jnp.int32, (cells, cells // 2), 0) // 2
    coarse = lax.broadcasted_iota(jnp.int32, (cells, cells // 2), 1)
    chosen = fine == coarse
    down = jnp.where(chosen, 0.25, 0.0).astype(bf16)
    up = jnp.where(chosen, 1.0, 0.0).astype(bf16).T
    wide = pltpu.VMEM((3, planes + 2, rows + 2 * channels, cells), bf16)
    small = (planes, rows // 2, cells // 2)
    dma = pltpu.SemaphoreType.DMA
    updated, grads = pl.pallas_call(
        functools.partial(kernel, n_tm, n_slab, chunk),
        out_shape=(
            jax.ShapeDtypeStruct((planes, rows, cells), f32),
            jax.ShapeDtypeStruct((n_slab, chunk, 4 * channels), f32),
        ),
        in_specs=[pl.BlockSpec(memory_space=pltpu.VMEM)] * 8,
        out_specs=[pl.BlockSpec(memory_space=pltpu.VMEM)] * 2,
        scratch_shapes=[
            wide, wide, wide, wide,
            pltpu.VMEM((4, 2, rows, cells), bf16),
            pltpu.VMEM((planes, rows, cells), f32),
            pltpu.VMEM((planes, rows, cells), f32),
            pltpu.VMEM((9, 2 * channels, 4 * channels), f32),
            pltpu.VMEM((2 * channels, cells), f32),
            pltpu.VMEM((2,) + small, bf16),
            pltpu.VMEM(small, bf16),
            pltpu.VMEM((n_tm - 1, 2) + small, bf16),
            pltpu.VMEM((n_tm - 1,) + small, bf16),
            pltpu.VMEM((n_slab * chunk, 4 * channels), bf16),
            pltpu.VMEM((n_slab - 1, chunk, 4 * channels), bf16),
            pltpu.VMEM((n_tm, chunk, 4 * channels), bf16),
            pltpu.VMEM((n_slab, chunk, 4 * channels), bf16),
            dma((4, 2)), dma((4, 2)),
            dma((n_tm - 1,)), dma((n_tm - 1,)), dma((n_tm - 1,)), dma((n_tm - 1,)),
            dma((n_slab - 1,)), dma((n_slab - 1,)),
            dma((n_tm - 1,)), dma((n_tm - 1,)),
            dma((n_slab - 1,)), dma((n_slab - 1,)),
        ],
        compiler_params=pltpu.CompilerParams(
            collective_id=0, has_side_effects=True, vmem_limit_bytes=56 * 2**20
        ),
        cost_estimate=pl.CostEstimate(flops=15 * 10**9, bytes_accessed=8 * 10**6, transcendentals=10**6),
    )(state, adjoint, forward, backward, offset, diagonal, down, up)
    lam_new = updated.reshape(planes, extent_x, channels, cells).transpose(2, 0, 1, 3)
    scale = step_size / math.sqrt(2 * n_tm * planes * n_slab * extent_x * cells)
    flat = grads.reshape(n_slab * chunk, 4 * channels)[: 9 * channels] * scale
    taps = flat[:, : 3 * channels].reshape(3, 3, channels, 3, channels)
    grad_w = taps.transpose(0, 3, 1, 2, 4).reshape(27, channels, channels)
    grad_b = flat[:channels, 3 * channels]
    return (lam_new[None], grad_w, grad_b)


def solution(mesh):
    in_specs = (P("tm", None, "slab", None, None), P("tm", None, "slab", None, None), P(), P())
    out_specs = (P("tm", None, "slab", None, None), P(), P())
    return jax.shard_map(
        on_device, mesh=mesh, in_specs=in_specs, out_specs=out_specs, check_vma=False
    )
```

```python
import functools
import math

import jax
import jax.numpy as jnp
from jax import lax
from jax.experimental import pallas as pl
from jax.experimental.pallas import tpu as pltpu
from jax.sharding import PartitionSpec as P

step_size = 0.25
MESH = pl.DeviceIdType.MESH
f32 = jnp.float32
bf16 = jnp.bfloat16


def kernel(
    n_tm, n_slab, chunk,
    u_ref, lam_ref, weight_ref, bias_ref,
    new_ref, grad_ref,
    wf_ref, wb_ref, down_ref, up_ref, partial,
    v0, v1, g1, g0, halo, sens0, mid, gacc, bacc,
    early, late, early_in, late_in, gsend, rs_in, tm_all, total,
    halo_send, halo_recv, early_send, early_recv, late_send, late_recv,
    rs_send, rs_recv, tm_send, tm_recv, ag_send, ag_recv,
):
    planes, rows, cells = u_ref.shape
    channels = rows // 8
    pair = 2 * channels
    pairs = rows // pair
    me_tm = lax.axis_index("tm")
    me = lax.axis_index("slab")

    def slab_peer(d):
        return lax.rem(me + d, n_slab)

    def tm_peer(d):
        return lax.rem(me_tm + d, n_tm)

    barrier = pltpu.get_barrier_semaphore()
    for d in range(1, n_slab):
        pl.semaphore_signal(barrier, inc=1, device_id={"slab": slab_peer(d)}, device_id_type=MESH)
    for d in range(1, n_tm):
        pl.semaphore_signal(barrier, inc=1, device_id={"tm": tm_peer(d)}, device_id_type=MESH)

    lane = lax.broadcasted_iota(jnp.int32, (pair, cells), 1)

    def put(buf, z, j, value):
        at = pl.ds(pl.multiple_of(channels + j * pair, channels), pair)
        wide = value.astype(f32)
        buf[1, z, at, :] = value
        buf[0, z, at, :] = jnp.where(lane == 0, 0.0, pltpu.roll(wide, 1, 1)).astype(bf16)
        buf[2, z, at, :] = jnp.where(lane == cells - 1, 0.0, pltpu.roll(wide, cells - 1, 1)).astype(bf16)

    def group(j):
        return pl.ds(pl.multiple_of(j * pair, pair), pair)

    def exchange(e, buf, start):
        own = pl.ds(channels, rows)

        def up():
            return pltpu.make_async_remote_copy(
                src_ref=buf.at[1, planes, own], dst_ref=halo.at[e, 0],
                send_sem=halo_send.at[e, 0], recv_sem=halo_recv.at[e, 0],
                device_id={"slab": jnp.minimum(me + 1, n_slab - 1)}, device_id_type=MESH)

        def down():
            return pltpu.make_async_remote_copy(
                src_ref=buf.at[1, 1, own], dst_ref=halo.at[e, 1],
                send_sem=halo_send.at[e, 1], recv_sem=halo_recv.at[e, 1],
                device_id={"slab": jnp.maximum(me - 1, 0)}, device_id_type=MESH)

        if start:
            @pl.when(me < n_slab - 1)
            def _():
                up().start()

            @pl.when(me > 0)
            def _():
                down().start()
        else:
            @pl.when(me > 0)
            def _():
                up().wait_recv()

                def move(j, carry):
                    put(buf, 0, j, halo[e, 0, group(j), :])
                    return carry
                lax.fori_loop(0, pairs, move, 0)

            @pl.when(me == 0)
            def _():
                buf[:, 0, :, :] = jnp.zeros_like(buf[:, 0, :, :])

            @pl.when(me < n_slab - 1)
            def _():
                down().wait_recv()

                def move(j, carry):
                    put(buf, planes + 1, j, halo[e, 1, group(j), :])
                    return carry
                lax.fori_loop(0, pairs, move, 0)

            @pl.when(me == n_slab - 1)
            def _():
                buf[:, planes + 1, :, :] = jnp.zeros_like(buf[:, planes + 1, :, :])

            @pl.when(me < n_slab - 1)
            def _():
                up().wait_send()

            @pl.when(me > 0)
            def _():
                down().wait_send()

    def window(j):
        return pl.ds(pl.multiple_of(j * pair, pair), 2 * pair)

    def inner(buf, taps, finish):
        def body(j, carry):
            acc = [None] * planes
            for source in range(1, planes + 1):
                used = [a for a in range(3) if 0 <= source - a < planes]
                low, high = used[0] * pair, (used[-1] + 1) * pair
                out = None
                for c in range(3):
                    product = jnp.dot(taps[c, low:high, :], buf[c, source, window(j), :],
                                      preferred_element_type=f32)
                    out = product if out is None else out + product
                for n, a in enumerate(used):
                    piece = out[n * pair:(n + 1) * pair]
                    z = source - a
                    acc[z] = piece if acc[z] is None else acc[z] + piece
                done = source - 2
                if 0 < done < planes - 1:
                    finish(done, j, acc[done])
            partial[0, group(j), :] = acc[0]
            partial[1, group(j), :] = acc[planes - 1]
            return carry
        lax.fori_loop(0, pairs, body, 0)

    def outer(buf, taps, finish):
        def body(j, carry):
            for n, (source, a) in enumerate(((0, 0), (planes + 1, 2))):
                acc = partial[n, group(j), :]
                for c in range(3):
                    acc = acc + jnp.dot(taps[c, a * pair:(a + 1) * pair, :],
                                        buf[c, source, window(j), :], preferred_element_type=f32)
                finish(source - a, j, acc)
            return carry
        lax.fori_loop(0, pairs, body, 0)

    def taps_grad(cot, buf):
        def body(j, carry):
            at = pl.ds(pl.multiple_of(channels + j * pair, channels), pair)
            for c in range(3):
                acc = [None] * 3
                for source in range(planes + 2):
                    used = [a for a in range(3) if 0 <= source - a < planes]
                    left = jnp.concatenate([cot[1, source - a + 1, at, :] for a in used], 0)
                    out = lax.dot_general(left, buf[c, source, window(j), :],
                                          (((1,), (1,)), ((), ())), preferred_element_type=f32)
                    for n, a in enumerate(used):
                        piece = out[n * pair:(n + 1) * pair]
                        acc[a] = piece if acc[a] is None else acc[a] + piece
                for a in range(3):
                    gacc[3 * a + c] += acc[a]
            return carry
        lax.fori_loop(0, pairs, body, 0)

    def restricted(value):
        summed = (value[:channels] + value[channels:]).astype(bf16)
        return jnp.dot(summed, down_ref[...], preferred_element_type=f32)

    def half(j):
        return pl.ds(pl.multiple_of(j * channels, channels), channels)

    def load_u(k, carry):
        j = lax.rem(k, pairs)
        z = k // pairs
        put(v0, z + 1, j, u_ref[z, group(j), :])
        return carry
    lax.fori_loop(0, planes * pairs, load_u, 0)

    def place(taps, a, b, c, block):
        taps[c, a * pair:a * pair + channels, b * channels:(b + 1) * channels] = block
        taps[c, a * pair + channels:(a + 1) * pair, (b + 1) * channels:(b + 2) * channels] = block

    wf_ref[...] = jnp.zeros_like(wf_ref)
    for a in range(3):
        for b in range(3):
            for c in range(3):
                place(wf_ref, a, b, c, weight_ref[9 * a + 3 * b + c])

    pl.semaphore_wait(barrier, n_slab - 1 + n_tm - 1)
    exchange(0, v0, True)

    wb_ref[...] = jnp.zeros_like(wb_ref)
    for a in range(3):
        for b in range(3):
            for c in range(3):
                block = weight_ref[26 - (9 * a + 3 * b + c)].astype(f32)
                place(wb_ref, a, b, c, block.T.astype(bf16))
    fine_at = lax.broadcasted_iota(jnp.int32, (cells, cells // 2), 0) // 2
    coarse_at = lax.broadcasted_iota(jnp.int32, (cells, cells // 2), 1)
    down_ref[...] = jnp.where(fine_at == coarse_at, 0.25, 0.0).astype(bf16)
    fine_at = lax.broadcasted_iota(jnp.int32, (cells // 2, cells), 1) // 2
    coarse_at = lax.broadcasted_iota(jnp.int32, (cells // 2, cells), 0)
    up_ref[...] = jnp.where(fine_at == coarse_at, 1.0, 0.0).astype(bf16)
    row = lax.rem(lax.broadcasted_iota(jnp.int32, (pair, channels), 0), channels)
    column_at = lax.broadcasted_iota(jnp.int32, (pair, channels), 1)
    offset = jnp.sum(jnp.where(row == column_at, bias_ref[...], 0.0), axis=1, keepdims=True)
    middle_tap = weight_ref[13].astype(f32)
    diagonal = jnp.sum(jnp.where((row == column_at)[:channels], middle_tap, 0.0), axis=1, keepdims=True)

    for buf in (v0, v1, g1, g0):
        for c in range(3):
            for z in range(planes + 2):
                buf[c, z, :channels, :] = jnp.zeros((channels, cells), bf16)
                buf[c, z, channels + rows:, :] = jnp.zeros((channels, cells), bf16)
    gacc[...] = jnp.zeros_like(gacc)
    bacc[...] = jnp.zeros_like(bacc)

    def after_first(z, j, acc):
        th = jnp.tanh(acc + offset)
        sens = 1.0 - th * th
        sens0[z, group(j), :] = sens
        state = (u_ref[z, group(j), :].astype(f32) + step_size * th).astype(bf16)
        put(v1, z + 1, j, state)
        early[0, z, half(j), :] = (1.0 + 2.0 * step_size * diagonal * restricted(sens)).astype(bf16)
        early[1, z, half(j), :] = restricted(lam_ref[z, group(j), :]).astype(bf16)

    inner(v0, wf_ref, after_first)
    exchange(0, v0, False)
    outer(v0, wf_ref, after_first)
    exchange(1, v1, True)

    def to_later(src, dst, send, recv, d):
        return pltpu.make_async_remote_copy(
            src_ref=src, dst_ref=dst.at[d - 1], send_sem=send.at[d - 1], recv_sem=recv.at[d - 1],
            device_id={"tm": jnp.minimum(me_tm + d, n_tm - 1)}, device_id_type=MESH)

    for d in range(1, n_tm):
        @pl.when(me_tm + d < n_tm)
        def _(d=d):
            to_later(early, early_in, early_send, early_recv, d).start()

    def after_second(z, j, acc):
        th = jnp.tanh(acc + offset)
        cot = ((1.0 - th * th) * lam_ref[z, group(j), :]).astype(bf16)
        bacc[...] += cot.astype(f32)
        put(g1, z + 1, j, cot)

    inner(v1, wf_ref, after_second)
    exchange(1, v1, False)
    outer(v1, wf_ref, after_second)
    exchange(2, g1, True)
    taps_grad(g1, v1)

    def after_third(z, j, acc):
        middle = lam_ref[z, group(j), :] + step_size * acc
        mid[z, group(j), :] = middle
        cot = (sens0[z, group(j), :] * middle).astype(bf16)
        bacc[...] += cot.astype(f32)
        put(g0, z + 1, j, cot)

    inner(g1, wb_ref, after_third)
    exchange(2, g1, False)
    outer(g1, wb_ref, after_third)
    exchange(3, g0, True)
    taps_grad(g0, v0)

    three = 3 * channels
    for t in range(9):
        block = gacc[t, :channels, :three] + gacc[t, channels:, channels:]
        gsend[t * channels:(t + 1) * channels, :three] = block.astype(bf16)
        side = jnp.zeros((channels, channels), f32)
        if t == 0:
            column = jnp.sum(bacc[:channels] + bacc[channels:], axis=1, keepdims=True)
            side = side + column
        gsend[t * channels:(t + 1) * channels, three:] = side.astype(bf16)
    padding = n_slab * chunk - 9 * channels
    if padding:
        gsend[9 * channels:, :] = jnp.zeros((padding, 4 * channels), bf16)

    def part(index):
        return pl.ds(pl.multiple_of(index * chunk, 16), chunk)

    def scatter(d):
        return pltpu.make_async_remote_copy(
            src_ref=gsend.at[part(slab_peer(d))], dst_ref=rs_in.at[d - 1],
            send_sem=rs_send.at[d - 1], recv_sem=rs_recv.at[d - 1],
            device_id={"slab": slab_peer(d)}, device_id_type=MESH)

    for d in range(1, n_slab):
        scatter(d).start()

    def after_fourth(z, j, acc):
        back = mid[z, group(j), :] + step_size * acc
        late[z, half(j), :] = restricted(back).astype(bf16)

    inner(g0, wb_ref, after_fourth)
    exchange(3, g0, False)
    outer(g0, wb_ref, after_fourth)

    for d in range(1, n_tm):
        @pl.when(me_tm + d < n_tm)
        def _(d=d):
            to_later(late, late_in, late_send, late_recv, d).start()

    mine = gsend[part(me), :].astype(f32)
    for d in range(1, n_slab):
        scatter(d).wait_recv()
        mine = mine + rs_in[d - 1].astype(f32)
    tm_all[me_tm] = mine.astype(bf16)

    def across(d):
        return pltpu.make_async_remote_copy(
            src_ref=tm_all.at[me_tm], dst_ref=tm_all.at[me_tm],
            send_sem=tm_send.at[d - 1], recv_sem=tm_recv.at[d - 1],
            device_id={"tm": tm_peer(d)}, device_id_type=MESH)

    for d in range(1, n_tm):
        across(d).start()
    for d in range(1, n_tm):
        across(d).wait_recv()
    whole = tm_all[0].astype(f32)
    for k in range(1, n_tm):
        whole = whole + tm_all[k].astype(f32)
    total[me] = whole.astype(bf16)

    def spread(d):
        return pltpu.make_async_remote_copy(
            src_ref=total.at[me], dst_ref=total.at[me],
            send_sem=ag_send.at[d - 1], recv_sem=ag_recv.at[d - 1],
            device_id={"slab": slab_peer(d)}, device_id_type=MESH)

    for d in range(1, n_slab):
        spread(d).start()

    for d in range(1, n_tm):
        @pl.when(me_tm >= d)
        def _(d=d):
            to_later(early, early_in, early_send, early_recv, d).wait_recv()
            to_later(late, late_in, late_send, late_recv, d).wait_recv()

    for d in range(n_tm):
        @pl.when(me_tm == d)
        def _(d=d):
            def body(k, carry):
                z = k // pairs
                j = lax.rem(k, pairs)
                at = half(j)
                first = early if d == 0 else early_in.at[d - 1]
                value = -first[1, z, at, :].astype(f32)
                for s in range(d, 0, -1):
                    lam_next = (early if s == 1 else early_in.at[s - 2])[1, z, at, :]
                    value = (early_in[s - 1, 0, z, at, :].astype(f32) * value
                             + late_in[s - 1, z, at, :].astype(f32) - lam_next.astype(f32))
                high = value.astype(bf16)
                low = (value - high.astype(f32)).astype(bf16)
                fine = (jnp.dot(high, up_ref[...], preferred_element_type=f32)
                        + jnp.dot(low, up_ref[...], preferred_element_type=f32))
                new_ref[z, group(j), :] = lam_ref[z, group(j), :] + jnp.concatenate([fine, fine], 0)
                return carry
            lax.fori_loop(0, planes * pairs, body, 0)

    for d in range(1, n_slab):
        spread(d).wait_recv()
    for s in range(n_slab):
        grad_ref[s] = total[s].astype(f32)

    for d in range(1, n_slab):
        scatter(d).wait_send()
        spread(d).wait_send()
    for d in range(1, n_tm):
        across(d).wait_send()

        @pl.when(me_tm + d < n_tm)
        def _(d=d):
            to_later(early, early_in, early_send, early_recv, d).wait_send()
            to_later(late, late_in, late_send, late_recv, d).wait_send()


def on_device(u_states, lam_points, weight, bias):
    n_tm, n_slab = lax.axis_size("tm"), lax.axis_size("slab")
    _, channels, planes, extent_x, cells = u_states.shape
    rows = channels * extent_x
    chunk = 16 * -(-9 * channels // (16 * n_slab))
    state = u_states[0].transpose(1, 2, 0, 3).reshape(planes, rows, cells)
    adjoint = lam_points[0].transpose(1, 2, 0, 3).reshape(planes, rows, cells)
    wide = pltpu.VMEM((3, planes + 2, rows + 2 * channels, cells), bf16)
    small = (planes, rows // 2, cells // 2)
    dma = pltpu.SemaphoreType.DMA
    updated, grads = pl.pallas_call(
        functools.partial(kernel, n_tm, n_slab, chunk),
        out_shape=(
            jax.ShapeDtypeStruct((planes, rows, cells), f32),
            jax.ShapeDtypeStruct((n_slab, chunk, 4 * channels), f32),
        ),
        in_specs=[pl.BlockSpec(memory_space=pltpu.VMEM)] * 4,
        out_specs=[pl.BlockSpec(memory_space=pltpu.VMEM)] * 2,
        scratch_shapes=[
            pltpu.VMEM((3, 6 * channels, 4 * channels), bf16),
            pltpu.VMEM((3, 6 * channels, 4 * channels), bf16),
            pltpu.VMEM((cells, cells // 2), bf16),
            pltpu.VMEM((cells // 2, cells), bf16),
            pltpu.VMEM((2, rows, cells), f32),
            wide, wide, wide, wide,
            pltpu.VMEM((4, 2, rows, cells), bf16),
            pltpu.VMEM((planes, rows, cells), f32),
            pltpu.VMEM((planes, rows, cells), f32),
            pltpu.VMEM((9, 2 * channels, 4 * channels), f32),
            pltpu.VMEM((2 * channels, cells), f32),
            pltpu.VMEM((2,) + small, bf16),
            pltpu.VMEM(small, bf16),
            pltpu.VMEM((n_tm - 1, 2) + small, bf16),
            pltpu.VMEM((n_tm - 1,) + small, bf16),
            pltpu.VMEM((n_slab * chunk, 4 * channels), bf16),
            pltpu.VMEM((n_slab - 1, chunk, 4 * channels), bf16),
            pltpu.VMEM((n_tm, chunk, 4 * channels), bf16),
            pltpu.VMEM((n_slab, chunk, 4 * channels), bf16),
            dma((4, 2)), dma((4, 2)),
            dma((n_tm - 1,)), dma((n_tm - 1,)), dma((n_tm - 1,)), dma((n_tm - 1,)),
            dma((n_slab - 1,)), dma((n_slab - 1,)),
            dma((n_tm - 1,)), dma((n_tm - 1,)),
            dma((n_slab - 1,)), dma((n_slab - 1,)),
        ],
        compiler_params=pltpu.CompilerParams(
            collective_id=0, has_side_effects=True, vmem_limit_bytes=56 * 2**20
        ),
        cost_estimate=pl.CostEstimate(flops=15 * 10**9, bytes_accessed=8 * 10**6, transcendentals=10**6),
    )(state, adjoint, weight, bias[None])
    lam_new = updated.reshape(planes, extent_x, channels, cells).transpose(2, 0, 1, 3)
    scale = step_size / math.sqrt(2 * n_tm * planes * n_slab * extent_x * cells)
    flat = grads.reshape(n_slab * chunk, 4 * channels)[: 9 * channels] * scale
    taps = flat[:, : 3 * channels].reshape(3, 3, channels, 3, channels)
    grad_w = taps.transpose(0, 3, 1, 2, 4).reshape(27, channels, channels)
    grad_b = flat[:channels, 3 * channels]
    return (lam_new[None], grad_w, grad_b)


def solution(mesh):
    in_specs = (P("tm", None, "slab", None, None), P("tm", None, "slab", None, None), P(), P())
    out_specs = (P("tm", None, "slab", None, None), P(), P())
    return jax.shard_map(
        on_device, mesh=mesh, in_specs=in_specs, out_specs=out_specs, check_vma=False
    )
```

```python
import functools
import math

import jax
import jax.numpy as jnp
from jax import lax
from jax.experimental import pallas as pl
from jax.experimental.pallas import tpu as pltpu
from jax.sharding import PartitionSpec as P

step_size = 0.25
MESH = pl.DeviceIdType.MESH
f32 = jnp.float32
bf16 = jnp.bfloat16


def kernel(
    n_tm, n_slab, chunk, scale,
    u_ref, lam_hbm, weight_ref, bias_ref,
    new_hbm, grad_ref, gbias_ref,
    lam_ref, new_ref, lam_sem, new_sem,
    wf_ref, wb_ref, down_ref, up_ref, partial,
    v0, v1, g1, g0, halo, sens0, mid, gacc, bacc,
    early, late, early_in, late_in, gsend, rs_in, tm_all, total,
    halo_send, halo_recv, early_send, early_recv, late_send, late_recv,
    rs_send, rs_recv, tm_send, tm_recv, ag_send, ag_recv,
):
    planes, rows, cells = u_ref.shape
    channels = rows // 8
    pair = 2 * channels
    pairs = rows // pair
    me_tm = lax.axis_index("tm")
    me = lax.axis_index("slab")

    def lam_copy(z, x):
        return pltpu.make_async_copy(
            lam_hbm.at[0, :, z, x, :], lam_ref.at[z, pl.ds(x * channels, channels), :], lam_sem.at[z, x])

    def new_copy(z, x):
        return pltpu.make_async_copy(
            new_ref.at[z, pl.ds(x * channels, channels), :], new_hbm.at[0, :, z, x, :], new_sem.at[z, x])

    everywhere = [(z, x) for z in range(planes) for x in range(8)]
    for z, x in everywhere:
        lam_copy(z, x).start()

    def slab_peer(d):
        return lax.rem(me + d, n_slab)

    def tm_peer(d):
        return lax.rem(me_tm + d, n_tm)

    barrier = pltpu.get_barrier_semaphore()
    for d in range(1, n_slab):
        pl.semaphore_signal(barrier, inc=1, device_id={"slab": slab_peer(d)}, device_id_type=MESH)
    for d in range(1, n_tm):
        pl.semaphore_signal(barrier, inc=1, device_id={"tm": tm_peer(d)}, device_id_type=MESH)

    lane = lax.broadcasted_iota(jnp.int32, (pair, cells), 1)

    def put(buf, z, j, value):
        at = pl.ds(pl.multiple_of(channels + j * pair, channels), pair)
        wide = value.astype(f32)
        buf[1, z, at, :] = value
        buf[0, z, at, :] = jnp.where(lane == 0, 0.0, pltpu.roll(wide, 1, 1)).astype(bf16)
        buf[2, z, at, :] = jnp.where(lane == cells - 1, 0.0, pltpu.roll(wide, cells - 1, 1)).astype(bf16)

    def group(j):
        return pl.ds(pl.multiple_of(j * pair, pair), pair)

    def exchange(e, buf, start):
        own = pl.ds(channels, rows)

        def up():
            return pltpu.make_async_remote_copy(
                src_ref=buf.at[1, planes, own], dst_ref=halo.at[e, 0],
                send_sem=halo_send.at[e, 0], recv_sem=halo_recv.at[e, 0],
                device_id={"slab": jnp.minimum(me + 1, n_slab - 1)}, device_id_type=MESH)

        def down():
            return pltpu.make_async_remote_copy(
                src_ref=buf.at[1, 1, own], dst_ref=halo.at[e, 1],
                send_sem=halo_send.at[e, 1], recv_sem=halo_recv.at[e, 1],
                device_id={"slab": jnp.maximum(me - 1, 0)}, device_id_type=MESH)

        if start:
            @pl.when(me < n_slab - 1)
            def _():
                up().start()

            @pl.when(me > 0)
            def _():
                down().start()
        else:
            @pl.when(me > 0)
            def _():
                up().wait_recv()

                def move(j, carry):
                    put(buf, 0, j, halo[e, 0, group(j), :])
                    return carry
                lax.fori_loop(0, pairs, move, 0)

            @pl.when(me == 0)
            def _():
                buf[:, 0, :, :] = jnp.zeros_like(buf[:, 0, :, :])

            @pl.when(me < n_slab - 1)
            def _():
                down().wait_recv()

                def move(j, carry):
                    put(buf, planes + 1, j, halo[e, 1, group(j), :])
                    return carry
                lax.fori_loop(0, pairs, move, 0)

            @pl.when(me == n_slab - 1)
            def _():
                buf[:, planes + 1, :, :] = jnp.zeros_like(buf[:, planes + 1, :, :])

            @pl.when(me < n_slab - 1)
            def _():
                up().wait_send()

            @pl.when(me > 0)
            def _():
                down().wait_send()

    def window(j):
        return pl.ds(pl.multiple_of(j * pair, pair), 2 * pair)

    def inner(buf, taps, finish):
        def body(j, carry):
            acc = [None] * planes
            for source in range(1, planes + 1):
                used = [a for a in range(3) if 0 <= source - a < planes]
                low, high = used[0] * pair, (used[-1] + 1) * pair
                out = None
                for c in range(3):
                    product = jnp.dot(taps[c, low:high, :], buf[c, source, window(j), :],
                                      preferred_element_type=f32)
                    out = product if out is None else out + product
                for n, a in enumerate(used):
                    piece = out[n * pair:(n + 1) * pair]
                    z = source - a
                    acc[z] = piece if acc[z] is None else acc[z] + piece
                done = source - 2
                if 0 < done < planes - 1:
                    finish(done, j, acc[done])
            partial[0, group(j), :] = acc[0]
            partial[1, group(j), :] = acc[planes - 1]
            return carry
        lax.fori_loop(0, pairs, body, 0)

    def outer(buf, taps, finish):
        def body(j, carry):
            for n, (source, a) in enumerate(((0, 0), (planes + 1, 2))):
                acc = partial[n, group(j), :]
                for c in range(3):
                    acc = acc + jnp.dot(taps[c, a * pair:(a + 1) * pair, :],
                                        buf[c, source, window(j), :], preferred_element_type=f32)
                finish(source - a, j, acc)
            return carry
        lax.fori_loop(0, pairs, body, 0)

    def taps_grad(cot, buf):
        def body(j, carry):
            at = pl.ds(pl.multiple_of(channels + j * pair, channels), pair)
            for c in range(3):
                acc = [None] * 3
                for source in range(planes + 2):
                    used = [a for a in range(3) if 0 <= source - a < planes]
                    left = jnp.concatenate([cot[1, source - a + 1, at, :] for a in used], 0)
                    out = lax.dot_general(left, buf[c, source, window(j), :],
                                          (((1,), (1,)), ((), ())), preferred_element_type=f32)
                    for n, a in enumerate(used):
                        piece = out[n * pair:(n + 1) * pair]
                        acc[a] = piece if acc[a] is None else acc[a] + piece
                for a in range(3):
                    gacc[3 * a + c] += acc[a]
            return carry
        lax.fori_loop(0, pairs, body, 0)

    def restricted(value):
        summed = (value[:channels] + value[channels:]).astype(bf16)
        return jnp.dot(summed, down_ref[...], preferred_element_type=f32)

    def half(j):
        return pl.ds(pl.multiple_of(j * channels, channels), channels)

    def load_u(k, carry):
        j = lax.rem(k, pairs)
        z = k // pairs
        put(v0, z + 1, j, u_ref[z, group(j), :])
        return carry
    lax.fori_loop(0, planes * pairs, load_u, 0)

    def place(taps, a, b, c, block):
        taps[c, a * pair:a * pair + channels, b * channels:(b + 1) * channels] = block
        taps[c, a * pair + channels:(a + 1) * pair, (b + 1) * channels:(b + 2) * channels] = block

    wf_ref[...] = jnp.zeros_like(wf_ref)
    for a in range(3):
        for b in range(3):
            for c in range(3):
                place(wf_ref, a, b, c, weight_ref[9 * a + 3 * b + c])

    pl.semaphore_wait(barrier, n_slab - 1 + n_tm - 1)
    exchange(0, v0, True)

    wb_ref[...] = jnp.zeros_like(wb_ref)
    for a in range(3):
        for b in range(3):
            for c in range(3):
                block = weight_ref[26 - (9 * a + 3 * b + c)].astype(f32)
                place(wb_ref, a, b, c, block.T.astype(bf16))
    fine_at = lax.broadcasted_iota(jnp.int32, (cells, cells // 2), 0) // 2
    coarse_at = lax.broadcasted_iota(jnp.int32, (cells, cells // 2), 1)
    down_ref[...] = jnp.where(fine_at == coarse_at, 0.25, 0.0).astype(bf16)
    fine_at = lax.broadcasted_iota(jnp.int32, (cells // 2, cells), 1) // 2
    coarse_at = lax.broadcasted_iota(jnp.int32, (cells // 2, cells), 0)
    up_ref[...] = jnp.where(fine_at == coarse_at, 1.0, 0.0).astype(bf16)
    row = lax.rem(lax.broadcasted_iota(jnp.int32, (pair, channels), 0), channels)
    column_at = lax.broadcasted_iota(jnp.int32, (pair, channels), 1)
    offset = jnp.sum(jnp.where(row == column_at, bias_ref[...], 0.0), axis=1, keepdims=True)
    middle_tap = weight_ref[13].astype(f32)
    diagonal = jnp.sum(jnp.where((row == column_at)[:channels], middle_tap, 0.0), axis=1, keepdims=True)

    for buf in (v0, v1, g1, g0):
        for c in range(3):
            for z in range(planes + 2):
                buf[c, z, :channels, :] = jnp.zeros((channels, cells), bf16)
                buf[c, z, channels + rows:, :] = jnp.zeros((channels, cells), bf16)
    gacc[...] = jnp.zeros_like(gacc)
    bacc[...] = jnp.zeros_like(bacc)

    def after_first(z, j, acc):
        th = jnp.tanh(acc + offset)
        sens = 1.0 - th * th
        sens0[z, group(j), :] = sens
        state = (u_ref[z, group(j), :].astype(f32) + step_size * th).astype(bf16)
        put(v1, z + 1, j, state)
        early[0, z, half(j), :] = (1.0 + 2.0 * step_size * diagonal * restricted(sens)).astype(bf16)
        early[1, z, half(j), :] = restricted(lam_ref[z, group(j), :]).astype(bf16)

    for z, x in everywhere:
        lam_copy(z, x).wait()
    inner(v0, wf_ref, after_first)
    exchange(0, v0, False)
    outer(v0, wf_ref, after_first)
    exchange(1, v1, True)

    def to_later(src, dst, send, recv, d):
        return pltpu.make_async_remote_copy(
            src_ref=src, dst_ref=dst.at[d - 1], send_sem=send.at[d - 1], recv_sem=recv.at[d - 1],
            device_id={"tm": jnp.minimum(me_tm + d, n_tm - 1)}, device_id_type=MESH)

    for d in range(1, n_tm):
        @pl.when(me_tm + d < n_tm)
        def _(d=d):
            to_later(early, early_in, early_send, early_recv, d).start()

    def after_second(z, j, acc):
        th = jnp.tanh(acc + offset)
        cot = ((1.0 - th * th) * lam_ref[z, group(j), :]).astype(bf16)
        bacc[...] += cot.astype(f32)
        put(g1, z + 1, j, cot)

    inner(v1, wf_ref, after_second)
    exchange(1, v1, False)
    outer(v1, wf_ref, after_second)
    exchange(2, g1, True)
    taps_grad(g1, v1)

    def after_third(z, j, acc):
        middle = lam_ref[z, group(j), :] + step_size * acc
        mid[z, group(j), :] = middle
        cot = (sens0[z, group(j), :] * middle).astype(bf16)
        bacc[...] += cot.astype(f32)
        put(g0, z + 1, j, cot)

    inner(g1, wb_ref, after_third)
    exchange(2, g1, False)
    outer(g1, wb_ref, after_third)
    exchange(3, g0, True)
    taps_grad(g0, v0)

    three = 3 * channels
    for t in range(9):
        block = gacc[t, :channels, :three] + gacc[t, channels:, channels:]
        gsend[t * channels:(t + 1) * channels, :three] = block.astype(bf16)
        side = jnp.zeros((channels, channels), f32)
        if t == 0:
            column = jnp.sum(bacc[:channels] + bacc[channels:], axis=1, keepdims=True)
            side = side + column
        gsend[t * channels:(t + 1) * channels, three:] = side.astype(bf16)
    padding = n_slab * chunk - 9 * channels
    if padding:
        gsend[9 * channels:, :] = jnp.zeros((padding, 4 * channels), bf16)

    def part(index):
        return pl.ds(pl.multiple_of(index * chunk, 16), chunk)

    def scatter(d):
        return pltpu.make_async_remote_copy(
            src_ref=gsend.at[part(slab_peer(d))], dst_ref=rs_in.at[d - 1],
            send_sem=rs_send.at[d - 1], recv_sem=rs_recv.at[d - 1],
            device_id={"slab": slab_peer(d)}, device_id_type=MESH)

    for d in range(1, n_slab):
        scatter(d).start()

    def after_fourth(z, j, acc):
        back = mid[z, group(j), :] + step_size * acc
        late[z, half(j), :] = restricted(back).astype(bf16)

    inner(g0, wb_ref, after_fourth)
    exchange(3, g0, False)
    outer(g0, wb_ref, after_fourth)

    for d in range(1, n_tm):
        @pl.when(me_tm + d < n_tm)
        def _(d=d):
            to_later(late, late_in, late_send, late_recv, d).start()

    mine = gsend[part(me), :].astype(f32)
    for d in range(1, n_slab):
        scatter(d).wait_recv()
        mine = mine + rs_in[d - 1].astype(f32)
    tm_all[me_tm] = mine.astype(bf16)

    def across(d):
        return pltpu.make_async_remote_copy(
            src_ref=tm_all.at[me_tm], dst_ref=tm_all.at[me_tm],
            send_sem=tm_send.at[d - 1], recv_sem=tm_recv.at[d - 1],
            device_id={"tm": tm_peer(d)}, device_id_type=MESH)

    for d in range(1, n_tm):
        across(d).start()
    for d in range(1, n_tm):
        across(d).wait_recv()
    whole = tm_all[0].astype(f32)
    for k in range(1, n_tm):
        whole = whole + tm_all[k].astype(f32)
    total[me] = whole.astype(bf16)

    def spread(d):
        return pltpu.make_async_remote_copy(
            src_ref=total.at[me], dst_ref=total.at[me],
            send_sem=ag_send.at[d - 1], recv_sem=ag_recv.at[d - 1],
            device_id={"slab": slab_peer(d)}, device_id_type=MESH)

    for d in range(1, n_slab):
        spread(d).start()

    for d in range(1, n_tm):
        @pl.when(me_tm >= d)
        def _(d=d):
            to_later(early, early_in, early_send, early_recv, d).wait_recv()
            to_later(late, late_in, late_send, late_recv, d).wait_recv()

    for d in range(n_tm):
        @pl.when(me_tm == d)
        def _(d=d):
            def body(k, carry):
                z = k // pairs
                j = lax.rem(k, pairs)
                at = half(j)
                first = early if d == 0 else early_in.at[d - 1]
                value = -first[1, z, at, :].astype(f32)
                for s in range(d, 0, -1):
                    lam_next = (early if s == 1 else early_in.at[s - 2])[1, z, at, :]
                    value = (early_in[s - 1, 0, z, at, :].astype(f32) * value
                             + late_in[s - 1, z, at, :].astype(f32) - lam_next.astype(f32))
                high = value.astype(bf16)
                low = (value - high.astype(f32)).astype(bf16)
                fine = (jnp.dot(high, up_ref[...], preferred_element_type=f32)
                        + jnp.dot(low, up_ref[...], preferred_element_type=f32))
                new_ref[z, group(j), :] = lam_ref[z, group(j), :] + jnp.concatenate([fine, fine], 0)
                return carry
            lax.fori_loop(0, planes * pairs, body, 0)

    for z, x in everywhere:
        new_copy(z, x).start()
    for d in range(1, n_slab):
        spread(d).wait_recv()
    summed = total[...].astype(f32).reshape(n_slab * chunk, 4 * channels) * scale
    for a in range(3):
        for c in range(3):
            t = 3 * a + c
            for b in range(3):
                grad_ref[9 * a + 3 * b + c] = summed[t * channels:(t + 1) * channels,
                                                     b * channels:(b + 1) * channels]
    gbias_ref[...] = jnp.sum(
        jnp.where((row == column_at)[:channels], summed[:channels, three:], 0.0), axis=0, keepdims=True)

    for d in range(1, n_slab):
        scatter(d).wait_send()
        spread(d).wait_send()
    for d in range(1, n_tm):
        across(d).wait_send()

        @pl.when(me_tm + d < n_tm)
        def _(d=d):
            to_later(early, early_in, early_send, early_recv, d).wait_send()
            to_later(late, late_in, late_send, late_recv, d).wait_send()
    for z, x in everywhere:
        new_copy(z, x).wait()


def on_device(u_states, lam_points, weight, bias):
    n_tm, n_slab = lax.axis_size("tm"), lax.axis_size("slab")
    _, channels, planes, extent_x, cells = u_states.shape
    rows = channels * extent_x
    chunk = 16 * -(-9 * channels // (16 * n_slab))
    state = u_states[0].transpose(1, 2, 0, 3).reshape(planes, rows, cells)
    scale = step_size / math.sqrt(2 * n_tm * planes * n_slab * extent_x * cells)
    wide = pltpu.VMEM((3, planes + 2, rows + 2 * channels, cells), bf16)
    small = (planes, rows // 2, cells // 2)
    dma = pltpu.SemaphoreType.DMA
    lam_new, grad_w, grad_b = pl.pallas_call(
        functools.partial(kernel, n_tm, n_slab, chunk, scale),
        out_shape=(
            jax.ShapeDtypeStruct(lam_points.shape, f32),
            jax.ShapeDtypeStruct((27, channels, channels), f32),
            jax.ShapeDtypeStruct((1, channels), f32),
        ),
        in_specs=[
            pl.BlockSpec(memory_space=pltpu.VMEM), pl.BlockSpec(memory_space=pl.ANY),
            pl.BlockSpec(memory_space=pltpu.VMEM), pl.BlockSpec(memory_space=pltpu.VMEM),
        ],
        out_specs=[
            pl.BlockSpec(memory_space=pl.ANY),
            pl.BlockSpec(memory_space=pltpu.VMEM), pl.BlockSpec(memory_space=pltpu.VMEM),
        ],
        scratch_shapes=[
            pltpu.VMEM((planes, rows, cells), f32),
            pltpu.VMEM((planes, rows, cells), f32),
            dma((planes, extent_x)), dma((planes, extent_x)),
            pltpu.VMEM((3, 6 * channels, 4 * channels), bf16),
            pltpu.VMEM((3, 6 * channels, 4 * channels), bf16),
            pltpu.VMEM((cells, cells // 2), bf16),
            pltpu.VMEM((cells // 2, cells), bf16),
            pltpu.VMEM((2, rows, cells), f32),
            wide, wide, wide, wide,
            pltpu.VMEM((4, 2, rows, cells), bf16),
            pltpu.VMEM((planes, rows, cells), f32),
            pltpu.VMEM((planes, rows, cells), f32),
            pltpu.VMEM((9, 2 * channels, 4 * channels), f32),
            pltpu.VMEM((2 * channels, cells), f32),
            pltpu.VMEM((2,) + small, bf16),
            pltpu.VMEM(small, bf16),
            pltpu.VMEM((n_tm - 1, 2) + small, bf16),
            pltpu.VMEM((n_tm - 1,) + small, bf16),
            pltpu.VMEM((n_slab * chunk, 4 * channels), bf16),
            pltpu.VMEM((n_slab - 1, chunk, 4 * channels), bf16),
            pltpu.VMEM((n_tm, chunk, 4 * channels), bf16),
            pltpu.VMEM((n_slab, chunk, 4 * channels), bf16),
            dma((4, 2)), dma((4, 2)),
            dma((n_tm - 1,)), dma((n_tm - 1,)), dma((n_tm - 1,)), dma((n_tm - 1,)),
            dma((n_slab - 1,)), dma((n_slab - 1,)),
            dma((n_tm - 1,)), dma((n_tm - 1,)),
            dma((n_slab - 1,)), dma((n_slab - 1,)),
        ],
        compiler_params=pltpu.CompilerParams(
            collective_id=0, has_side_effects=True, vmem_limit_bytes=56 * 2**20
        ),
        cost_estimate=pl.CostEstimate(flops=15 * 10**9, bytes_accessed=8 * 10**6, transcendentals=10**6),
    )(state, lam_points, weight, bias[None])
    return (lam_new, grad_w, grad_b[0])


def solution(mesh):
    in_specs = (P("tm", None, "slab", None, None), P("tm", None, "slab", None, None), P(), P())
    out_specs = (P("tm", None, "slab", None, None), P(), P())
    return jax.shard_map(
        on_device, mesh=mesh, in_specs=in_specs, out_specs=out_specs, check_vma=False
    )
```
